32 devices in a mesh: bead: 4 (over y, x), slab: 8 (over z, core).
Axes of the slice: x: 2, y: 2, z: 4, core: 2. Of those that a mesh axis runs over, the one named last changes fastest.
Arguments:
- section_modes: float32 [3, 8, 4096], P(None, 'bead', 'slab'), may hold values from -3 to 3
- velocity: float32 [3, 8, 4096], P(None, 'bead', 'slab'), may hold values from -6 to 6
- acceleration: float32 [3, 8, 4096], P(None, 'bead', 'slab'), may hold values from -6 to 6
- species: int32 [4096], P('slab'), may hold values from 0 to 1
- neighbours: int32 [32, 4096], P(None, 'slab'), may hold values from 0 to 896, as said below
- ghost_send: int32 [8, 384], P('slab'), may hold values from 0 to 511
Outputs:
- next_modes: float32 [3, 8, 4096], P(None, 'bead', 'slab')
- next_velocity: float32 [3, 8, 4096], P(None, 'bead', 'slab')
- next_acceleration: float32 [3, 8, 4096], P(None, 'bead', 'slab')
The draws below stay inside these ranges and needn't reach their ends.
Inputs may be any that keep to these rules, and one draw needn't show every extreme that they name: `neighbours`: A slot names the left neighbour slab's ghost block (192 entries), then the slab's own 512 atoms, then the right neighbour's ghost block; the value 512 + 2 * 192 marks an empty slot. `ghost_send`: row s lists first the 192 atoms of slab s that slab s - 1 holds as ghosts, then the 192 atoms that slab s + 1 holds.
All inputs are finite; a program needn't handle non-finite values.
Results may differ from the reference program's by a relative error of at most 0.000092.
Values sent between devices are 32-bit elements; how exact they have to be, the bound alone decides.
A program may use at most 64 MiB of HBM per device.

```python
import math
import jax
import jax.numpy as jnp
import numpy as np
from jax import lax

BEAD_DEV = 2
ATOM_DEV = 512
SLOTS = 32
GHOST = 192
BEADS = 8
ATOMS = 4096
N_BEAD = 4
N_SLAB = 8


def draw_neighbours(key, part):
    key = jax.random.fold_in(key, 7)
    index_key, empty_key = jax.random.split(key)
    slot_span = ATOM_DEV + 2 * GHOST
    picked = jax.random.randint(index_key, (SLOTS, ATOMS), 0, slot_span, dtype=jnp.int32)
    vacant = jax.random.randint(empty_key, (SLOTS, ATOMS), 0, 4, dtype=jnp.int32) == 0
    row_ids = lax.broadcasted_iota(jnp.int32, (SLOTS, ATOMS), 0)
    column_ids = lax.broadcasted_iota(jnp.int32, (SLOTS, ATOMS), 1)
    forced = (row_ids == SLOTS - 1) & (column_ids % 4 == 0)
    lowest = (row_ids == 0) & (column_ids % 64 == 1)
    filled = jnp.where(vacant | forced, slot_span, picked)
    return jnp.where(lowest, 0, filled).astype(jnp.int32)


def with_ends(result, rng, smallest, top_value):
    longest = result.shape.index(max(result.shape))
    spots = []
    for shift in (0, 1):
        where = [jax.random.randint(jax.random.fold_in(rng, axis), (), 0, length) for axis, length in enumerate(result.shape)]
        where[longest] = (where[longest] + shift) % result.shape[longest]
        spots.append(tuple(where))
    return result.at[spots[0]].set(smallest).at[spots[1]].set(top_value)


def block_levels(rng, dims, shards, low, top_value):
    def one(dim, shards_of):
        draws = jax.random.uniform(jax.random.fold_in(jax.random.fold_in(rng, 6), dim), (shards_of,), jnp.float32, low / len(shards), top_value / len(shards))
        return jnp.repeat(jnp.exp(draws), dims[dim] // shards_of).reshape((-1,) + (1,) * (len(dims) - dim - 1))

    loudness = one(*shards[0])
    for cut in shards[1:]:
        loudness = loudness * one(*cut)
    return loudness


def normal_values(rng, extent, scale, limit, cuts=(), kind=jnp.bfloat16):
    factor_of = block_levels(rng, extent, cuts, -0.22, 0.18) if cuts else 1.0
    result = jax.random.normal(rng, extent, jnp.float32) * scale * factor_of
    return jnp.minimum(jnp.maximum(result, -limit), limit).astype(kind)


def setup_inputs(seed: int = 0) -> dict:
    seeds = jax.random.split(jax.random.key(seed), 7)
    section_modes = normal_values(seeds[0], (3, BEADS, ATOMS), 0.4, 3.0, ((1, 4), (2, 8)), jnp.float32)
    velocity = normal_values(seeds[1], (3, BEADS, ATOMS), 1.0, 6.0, ((1, 4), (2, 8)), jnp.float32)
    acceleration = normal_values(seeds[2], (3, BEADS, ATOMS), 1.0, 6.0, ((1, 4), (2, 8)), jnp.float32)
    species = with_ends(jax.random.randint(seeds[3], (ATOMS,), 0, 2), jax.random.fold_in(seeds[3], 1), 0, 1).astype(jnp.int32)
    neighbours = draw_neighbours(jax.random.fold_in(seeds[6], 71), 0)
    ghost_send = with_ends(jax.random.randint(seeds[5], (N_SLAB, 2 * GHOST), 0, ATOM_DEV), jax.random.fold_in(seeds[5], 1), 0, ATOM_DEV - 1).astype(jnp.int32)
    return dict(section_modes=section_modes, velocity=velocity, acceleration=acceleration, species=species, neighbours=neighbours, ghost_send=ghost_send)


step_dt = 0.1
spring = 6.0
alpha_shape = 0.3
beta_shape = 0.5

def sectioning_inverse(number):
    row_table = np.zeros((number, number))
    row_table[0, 0] = 1.0
    for mode_level in range(number - 1, 0, -1):
        upper_row = row_table[0] if mode_level + 1 == number else row_table[mode_level + 1]
        row_table[mode_level] = mode_level / (mode_level + 1.0) * upper_row + 1.0 / (mode_level + 1.0) * row_table[0]
        row_table[mode_level, mode_level] += 1.0
    return row_table

def force_matrix(number):
    inverse = sectioning_inverse(number)
    weights = np.array([1.0] + [mode_level / (mode_level + 1.0) for mode_level in range(1, number)])
    return weights[:, None] * inverse.T / number

def species_values(species, light_value, heavy_value):
    return jnp.where(species == 1, heavy_value, light_value).astype(jnp.float32)

def propagate(mode_rows, velocity, acceleration, first_mode):
    half_kick = velocity + 0.5 * step_dt * acceleration
    turn_angle = spring * step_dt
    cosine = math.cos(turn_angle)
    sine_turn = math.sin(turn_angle)
    new_modes = jnp.where(first_mode, mode_rows + step_dt * half_kick, cosine * mode_rows + sine_turn / spring * half_kick)
    turned = jnp.where(first_mode, half_kick, cosine * half_kick - spring * sine_turn * mode_rows)
    return (new_modes, turned)

def partner_table(neighbours, ghost_send):
    atom_count = ATOM_DEV
    ghost_count = GHOST
    slab_ids = jnp.arange(N_SLAB, dtype=jnp.int32)
    left_slab = ((slab_ids - 1) % N_SLAB).astype(jnp.int32)
    right_slab = ((slab_ids + 1) % N_SLAB).astype(jnp.int32)
    from_left = left_slab[:, None] * atom_count + ghost_send[left_slab, ghost_count:]
    own_rows = slab_ids[:, None] * atom_count + jnp.arange(atom_count, dtype=jnp.int32)[None, :]
    from_right = right_slab[:, None] * atom_count + ghost_send[right_slab, :ghost_count]
    empty_slot = jnp.full((N_SLAB, 1), ATOMS, jnp.int32)
    lookup = jnp.concatenate([from_left, own_rows, from_right, empty_slot], axis=1).astype(jnp.int32)
    slot_span = atom_count + 2 * ghost_count + 1
    column_slab = (jnp.arange(ATOMS, dtype=jnp.int32) // atom_count).astype(jnp.int32)
    return lookup.reshape(-1)[(column_slab * slot_span)[None, :] + neighbours].astype(jnp.int32)

def bead_forces(bead_place, amplitude, repulsion, embedding, partner):
    atom_total = bead_place.shape[1]
    extended = jnp.concatenate([bead_place, jnp.zeros((3, 1), bead_place.dtype)], axis=1)
    amp_ext = jnp.concatenate([amplitude, jnp.zeros((1,), amplitude.dtype)])
    rep_ext = jnp.concatenate([repulsion, jnp.zeros((1,), repulsion.dtype)])
    offset = bead_place[:, None, :] - extended[:, partner]
    distance = lax.optimization_barrier(jnp.sum(offset * offset, axis=0))
    density_term = jnp.exp(-alpha_shape * distance)
    repel_term = jnp.exp(-beta_shape * distance)
    partner_amp = amp_ext[partner]
    flat_slots = partner.reshape(-1)
    density = lax.optimization_barrier(jnp.sum(partner_amp * density_term, axis=0)) + jax.ops.segment_sum((amplitude[None, :] * density_term).reshape(-1), flat_slots, atom_total + 1)[:atom_total]
    slope_rows = -embedding / (2.0 * jnp.sqrt(1.0 + density))
    slope_ext = jnp.concatenate([slope_rows, jnp.zeros((1,), slope_rows.dtype)])
    coupling = 2.0 * (alpha_shape * density_term * (slope_rows[None, :] * partner_amp + slope_ext[partner] * amplitude[None, :]) + beta_shape * repulsion[None, :] * rep_ext[partner] * repel_term)
    pair_force = coupling[None] * offset
    returned = jax.ops.segment_sum(pair_force.reshape(3, -1).T, flat_slots, atom_total + 1)[:atom_total].T
    return lax.optimization_barrier(jnp.sum(pair_force, axis=1)) - returned

def reference(section_modes, velocity, acceleration, species, neighbours, ghost_send):
    number = BEAD_DEV * N_BEAD
    first_mode = (jnp.arange(number, dtype=jnp.int32) == 0)[None, :, None]
    new_modes, turned = propagate(section_modes, velocity, acceleration, first_mode)
    inverse = jnp.asarray(sectioning_inverse(number), jnp.float32)
    positions = jnp.einsum('kj,cjn->ckn', inverse, new_modes, precision=lax.Precision.HIGHEST)
    amplitude = species_values(species, 0.6, 1.4)
    repulsion = species_values(species, 0.8, 1.5)
    embedding = species_values(species, 1.0, 2.5)
    inverse_mass = species_values(species, 1.0, 1.0 / 106.0)
    partner = partner_table(neighbours, ghost_send)

    def one_bead(bead_place):
        return bead_forces(bead_place, amplitude, repulsion, embedding, partner)
    forces = jnp.moveaxis(lax.map(one_bead, jnp.moveaxis(positions, 1, 0)), 0, 1)
    matrix = jnp.asarray(force_matrix(number), jnp.float32)
    new_accel = jnp.einsum('jk,ckn->cjn', matrix, forces, precision=lax.Precision.HIGHEST) * inverse_mass[None, None, :]
    new_velocity = turned + 0.5 * step_dt * new_accel
    return (new_modes, new_velocity, new_accel)
```

```python
import functools
import math

import jax
import jax.numpy as jnp
import numpy as np
from jax import lax
from jax.experimental import pallas as pl
from jax.experimental.pallas import tpu as pltpu
from jax.sharding import PartitionSpec as P

step_dt = 0.1
spring = 6.0
alpha_shape = 0.3
beta_shape = 0.5
log2e = math.log2(math.e)
MESH = pl.DeviceIdType.MESH
f32 = jnp.float32
bf16 = jnp.bfloat16


def sectioning_inverse(number):
    row_table = np.zeros((number, number))
    row_table[0, 0] = 1.0
    for mode_level in range(number - 1, 0, -1):
        upper_row = row_table[0] if mode_level + 1 == number else row_table[mode_level + 1]
        row_table[mode_level] = (
            mode_level / (mode_level + 1.0) * upper_row + 1.0 / (mode_level + 1.0) * row_table[0]
        )
        row_table[mode_level, mode_level] += 1.0
    return row_table


def force_matrix(number):
    inverse = sectioning_inverse(number)
    weights = np.array([1.0] + [mode_level / (mode_level + 1.0) for mode_level in range(1, number)])
    return weights[:, None] * inverse.T / number


def split_rows(rows):
    high = rows.astype(bf16).astype(f32)
    rest = rows - high
    middle = rest.astype(bf16).astype(f32)
    return jnp.concatenate([high, middle, rest - middle], axis=0).astype(bf16)


def fold_pieces(product):
    return product[0:8] + product[8:16] + product[16:24]


def row_dot(rows, table):
    return fold_pieces(
        lax.dot_general(
            split_rows(rows), table, (((1,), (0,)), ((), ())), preferred_element_type=f32
        )
    )


def row_dot_nt(rows, table):
    return fold_pieces(
        lax.dot_general(
            split_rows(rows), table, (((1,), (1,)), ((), ())), preferred_element_type=f32
        )
    )


def lane_sums(selector, partial):
    high = partial.astype(bf16)
    rest = partial - high.astype(f32)
    middle = rest.astype(bf16)
    low = (rest - middle.astype(f32)).astype(bf16)
    total = None
    for piece in (high, middle, low):
        part = lax.dot_general(
            selector, piece, (((1,), (1,)), ((), ())), preferred_element_type=f32
        )
        total = part if total is None else total + part
    return total


def choose(index, table_values):
    value = f32(table_values[0])
    for i in range(1, len(table_values)):
        value = jnp.where(index == i, f32(table_values[i]), value)
    return value


def kernel(
    sizes,
    modes_ref,
    vel_ref,
    acc_ref,
    spec_ref,
    nb_ref,
    ghost_ref,
    out_modes,
    out_vel,
    out_acc,
    lo_ref,
    inc_ref,
    count_ref,
    turned_ref,
    onehot_ref,
    modes_all,
    send_modes,
    place_ref,
    column_ref,
    dens_ref,
    rep_ref,
    part_d,
    part_f,
    send_d,
    got_d,
    send_s,
    got_s,
    slope_ref,
    slope_col,
    send_f,
    force_all,
    mixed_ref,
    sem_a,
    rem_a,
    sem_b,
    rem_b,
    sem_c,
    rem_c,
    sem_f,
    rem_f,
):
    nbead, nslab, beads, atoms, ghosts, pad, slots = sizes
    number = nbead * beads
    b = lax.axis_index("bead")
    s = lax.axis_index("slab")
    left = lax.rem(s + nslab - 1, nslab)
    right = lax.rem(s + 1, nslab)

    barrier = pltpu.get_barrier_semaphore()
    peers = []
    for d in range(nbead):
        t = lax.rem(b + d, nbead)
        if d:
            peers.append((t, s))
        peers.append((t, left))
        peers.append((t, right))
    for peer in peers:
        pl.semaphore_signal(barrier, inc=1, device_id=peer, device_id_type=MESH)

    def remote(src, dst, sems, rems, index, device):
        return pltpu.make_async_remote_copy(
            src_ref=src,
            dst_ref=dst,
            send_sem=sems.at[index],
            recv_sem=rems.at[index],
            device_id=device,
            device_id_type=MESH,
        )

    shape = (3, beads, atoms)
    first_mode = (lax.broadcasted_iota(jnp.int32, shape, 1) + b * beads) == 0
    modes = modes_ref[...]
    half_kick = vel_ref[...] + 0.5 * step_dt * acc_ref[...]
    angle = spring * step_dt
    cosine, sine = math.cos(angle), math.sin(angle)
    new_modes = jnp.where(
        first_mode, modes + step_dt * half_kick, cosine * modes + sine / spring * half_kick
    )
    turned_ref[...] = jnp.where(
        first_mode, half_kick, cosine * half_kick - spring * sine * modes
    )
    out_modes[...] = new_modes
    heavy = spec_ref[...] == 1
    for c in range(3):
        modes_all[b, c * beads : (c + 1) * beads, 0:atoms] = new_modes[c]
    modes_all[b, 6:7, 0:atoms] = jnp.where(heavy, f32(1.4), f32(0.6))
    modes_all[b, 7:8, 0:atoms] = jnp.where(heavy, f32(1.5), f32(0.8))

    listed = ghost_ref[...]
    lane = lax.broadcasted_iota(jnp.int32, (1, pad), 1)
    first_list = jnp.where(lane < ghosts, listed[:, 0:pad], -1)
    start = 2 * ghosts - pad
    second_list = jnp.where(
        lane < ghosts,
        pltpu.roll(
            jnp.broadcast_to(listed[:, start : start + pad], (8, pad)),
            pad - (ghosts - start),
            1,
        )[0:1],
        -1,
    )
    atom_ids = lax.broadcasted_iota(jnp.int32, (atoms, pad), 0)
    onehot_ref[:, 0:pad] = jnp.where(atom_ids == first_list, f32(1), f32(0)).astype(bf16)
    onehot_ref[:, pad : 2 * pad] = jnp.where(atom_ids == second_list, f32(1), f32(0)).astype(bf16)
    send_modes[...] = row_dot(modes_all[b, :, 0:atoms], onehot_ref[...])

    pl.semaphore_wait(barrier, len(peers))

    left_at = slice(atoms, atoms + pad)
    right_at = slice(atoms + pad, atoms + 2 * pad)

    def exchange(own_ref, src_left, src_right, buffer, at_left, at_right, sems, rems):
        copies = []
        for d in range(nbead):
            t = lax.rem(b + d, nbead)
            copies.append(
                remote(src_left, buffer.at[b, :, at_left], sems, rems, nbead + d, (t, left))
            )
            copies.append(
                remote(src_right, buffer.at[b, :, at_right], sems, rems, 2 * nbead + d, (t, right))
            )
            if d:
                copies.append(
                    remote(own_ref, buffer.at[b, :, 0:atoms], sems, rems, d, (t, s))
                )
        for copy in copies:
            copy.start()
        return copies

    copies_a = exchange(
        modes_all.at[b, :, 0:atoms],
        send_modes.at[:, 0:pad],
        send_modes.at[:, pad : 2 * pad],
        modes_all,
        right_at,
        left_at,
        sem_a,
        rem_a,
    )

    rows = atoms + 2 * pad
    field = rows // 4
    value = nb_ref[...]
    moved = jnp.where(
        value < ghosts,
        value + atoms,
        jnp.where(value < ghosts + atoms, value - ghosts, value - ghosts + pad),
    )
    level = (
        jnp.where(moved >= field, 1, 0)
        + jnp.where(moved >= 2 * field, 1, 0)
        + jnp.where(moved >= 3 * field, 1, 0)
    )
    lo_ref[...] = moved - level * field
    step = jnp.where(
        level == 0, 1, jnp.where(level == 1, 1 << 8, jnp.where(level == 2, 1 << 16, 1 << 24))
    )
    inc_ref[...] = jnp.where(value < atoms + 2 * ghosts, step, 0)
    group = 32
    row_ids = lax.broadcasted_iota(jnp.int32, (group, atoms), 0)

    def count_body(g, carry):
        base = g * group
        total = jnp.zeros((group, atoms), jnp.int32)
        for k in range(slots):
            total = total + jnp.where(
                row_ids == lo_ref[k : k + 1, :] - base, inc_ref[k : k + 1, :], 0
            )
        for level_id in range(4):
            at = pl.multiple_of(level_id * field + base, group)
            count_ref[pl.ds(at, group), :] = (
                (total >> (8 * level_id)) & 255
            ).astype(f32)
        return carry

    lax.fori_loop(0, field // group, count_body, 0)

    for side in range(2):
        at = atoms + side * pad + ghosts
        blank = jnp.zeros((pad - ghosts, 128), f32)
        for kk in range(beads):
            part_d[kk, at : at + pad - ghosts, :] = blank
            for c in range(3):
                part_f[kk * 3 + c, at : at + pad - ghosts, :] = blank

    sub_ids = lax.broadcasted_iota(jnp.int32, (8, 1), 0)

    def mix(buffer, matrix, kk):
        total = None
        for n in range(nbead):
            column = None
            for j in range(beads):
                coef = choose(
                    b, [matrix[i * beads + kk, n * beads + j] for i in range(nbead)]
                )
                column = (
                    jnp.full((8, 1), coef, f32)
                    if column is None
                    else jnp.where(lax.rem(sub_ids, beads) == j, coef, column)
                )
            part = column * buffer[n]
            total = part if total is None else total + part
        result = total
        for j in range(1, beads):
            result = result + pltpu.roll(total, 8 - j, 0)
        return result

    inverse = sectioning_inverse(number).astype(np.float32)
    for copy in copies_a:
        copy.wait_recv()
    place_ref[6:8, :] = modes_all[b, 6:8, :]
    for kk in range(beads):
        mixed = mix(modes_all, inverse, kk)
        for c in range(3):
            place_ref[kk * 3 + c : kk * 3 + c + 1, :] = mixed[c * beads : c * beads + 1, :]
    column_ref[...] = jnp.transpose(place_ref[...])

    def rows_of(index):
        return jnp.broadcast_to(place_ref[index : index + 1, 0:atoms], (8, atoms))

    def fold_lanes(full):
        out = full[:, 0:128]
        for at in range(128, atoms, 128):
            out = out + full[:, at : at + 128]
        return out

    unroll = 2

    def density_pass(kk, first_row, count, total):
        xn = [rows_of(kk * 3 + c) for c in range(3)]
        amp_n, rep_n = rows_of(6), rows_of(7)

        def body(i, total):
            for u in range(unroll):
                at = pl.multiple_of(first_row + (i * unroll + u) * 8, 8)
                here = pl.ds(at, 8)
                cols = column_ref[here, :]
                offset = [xn[c] - cols[:, kk * 3 + c : kk * 3 + c + 1] for c in range(3)]
                distance = (
                    offset[0] * offset[0] + offset[1] * offset[1] + offset[2] * offset[2]
                )
                listed_times = count_ref[here, :]
                dens = listed_times * jnp.exp2((-alpha_shape * log2e) * distance)
                repel = listed_times * jnp.exp2((-beta_shape * log2e) * distance)
                dens_ref[kk, here, :] = dens
                rep_ref[kk, here, :] = repel * (rep_n * cols[:, 7:8])
                part_d[kk, here, :] = fold_lanes(dens * amp_n)
                total = total + dens * cols[:, 6:7]
            return total

        return lax.fori_loop(0, count // (8 * unroll), body, total)

    ones = jnp.ones((8, 128), bf16)
    sides = (slice(atoms, atoms + pad), slice(atoms + pad, atoms + 2 * pad))
    totals = []
    copies_b = []
    for kk in range(beads):
        total = jnp.zeros((8, atoms), f32)
        for side in range(2):
            total = density_pass(kk, atoms + side * pad, ghosts, total)
            send_d[kk, :, side * pad : (side + 1) * pad] = lane_sums(
                ones, part_d[kk, sides[side], :]
            )
        pair = [
            remote(
                send_d.at[kk, :, 0:pad],
                got_d.at[kk, :, pad : 2 * pad],
                sem_b,
                rem_b,
                2 * kk,
                (b, left),
            ),
            remote(
                send_d.at[kk, :, pad : 2 * pad],
                got_d.at[kk, :, 0:pad],
                sem_b,
                rem_b,
                2 * kk + 1,
                (b, right),
            ),
        ]
        for copy in pair:
            copy.start()
        copies_b.append(pair)
        totals.append(total)
    locals_d = []
    for kk in range(beads):
        total = density_pass(kk, 0, atoms, totals[kk])
        locals_d.append(
            jnp.sum(total, axis=0, keepdims=True) + lane_sums(ones, part_d[kk, 0:atoms, :])
        )
    embed = jnp.where(heavy, f32(2.5), f32(1.0))
    copies_c = []
    for kk in range(beads):
        for copy in copies_b[kk]:
            copy.wait_recv()
        density = locals_d[kk] + row_dot_nt(got_d[kk], onehot_ref[...])
        slope = (-0.5 * 2.0 * alpha_shape) * embed / jnp.sqrt(1.0 + density)
        slope_ref[kk] = slope
        send_s[kk] = row_dot(slope, onehot_ref[...])
        pair = [
            remote(
                send_s.at[kk, :, 0:pad],
                got_s.at[kk, :, pad : 2 * pad],
                sem_c,
                rem_c,
                2 * kk,
                (b, left),
            ),
            remote(
                send_s.at[kk, :, pad : 2 * pad],
                got_s.at[kk, :, 0:pad],
                sem_c,
                rem_c,
                2 * kk + 1,
                (b, right),
            ),
        ]
        for copy in pair:
            copy.start()
        copies_c.append(pair)
        slope_col[kk, 0:atoms, :] = jnp.transpose(slope)

    def force_pass(kk, first_row, count, carry):
        xn = [rows_of(kk * 3 + c) for c in range(3)]
        amp_n = rows_of(6)
        slope_n = slope_ref[kk]

        def body(i, totals):
            for u in range(unroll):
                at = pl.multiple_of(first_row + (i * unroll + u) * 8, 8)
                here = pl.ds(at, 8)
                cols = column_ref[here, :]
                slope_m = slope_col[kk, here, :][:, 0:1]
                coupling = (
                    dens_ref[kk, here, :] * (slope_n * cols[:, 6:7] + amp_n * slope_m)
                    + rep_ref[kk, here, :]
                )
                out = []
                for c in range(3):
                    pair_force = coupling * (xn[c] - cols[:, kk * 3 + c : kk * 3 + c + 1])
                    part_f[kk * 3 + c, here, :] = fold_lanes(pair_force)
                    out.append(totals[c] + pair_force)
                totals = tuple(out)
            return totals

        return lax.fori_loop(0, count // (8 * unroll), body, carry)

    selector_ids = lax.broadcasted_iota(jnp.int32, (8, 128), 0)
    line_ids = lax.broadcasted_iota(jnp.int32, (8, atoms), 0)
    zero = jnp.zeros((8, atoms), f32)
    local_totals = [force_pass(kk, 0, atoms, (zero, zero, zero)) for kk in range(beads)]
    own = zero
    for kk in range(beads):
        for copy in copies_c[kk]:
            copy.wait_recv()
        slope_col[kk, atoms:rows, :] = jnp.transpose(got_s[kk])
        total = local_totals[kk]
        for side in range(2):
            total = force_pass(kk, atoms + side * pad, ghosts, total)
        for c in range(3):
            line = jnp.sum(total[c], axis=0, keepdims=True)
            own = own + jnp.where(line_ids == c * beads + kk, line, 0.0)
    sent = jnp.zeros((8, rows), f32)
    for kk in range(beads):
        for c in range(3):
            selector = jnp.where(selector_ids == c * beads + kk, f32(-1), f32(0)).astype(bf16)
            sent = sent + lane_sums(selector, part_f[kk * 3 + c])
    force_all[b, :, 0:atoms] = own + sent[:, 0:atoms]
    send_f[...] = sent[:, atoms:rows]
    copies_f = exchange(
        force_all.at[b, :, 0:atoms],
        send_f.at[:, 0:pad],
        send_f.at[:, pad : 2 * pad],
        force_all,
        right_at,
        left_at,
        sem_f,
        rem_f,
    )
    for copy in copies_a:
        copy.wait_send()
    for copy in sum(copies_b, []) + sum(copies_c, []):
        copy.wait_send()
    matrix = force_matrix(number).astype(np.float32)
    inverse_mass = jnp.where(heavy, f32(1.0 / 106.0), f32(1.0))
    for copy in copies_f:
        copy.wait_recv()
    mixed_ref[6:8, :] = jnp.zeros((2, rows), f32)
    for kk in range(beads):
        mixed = mix(force_all, matrix, kk)
        for c in range(3):
            at = c * beads + kk
            mixed_ref[at : at + 1, :] = mixed[c * beads : c * beads + 1, :]
    accel = (
        mixed_ref[:, 0:atoms] + row_dot_nt(mixed_ref[:, atoms:rows], onehot_ref[...])
    ) * inverse_mass
    for c in range(3):
        piece = accel[c * beads : (c + 1) * beads]
        out_acc[c] = piece
        out_vel[c] = turned_ref[c] + 0.5 * step_dt * piece
    for copy in copies_f:
        copy.wait_send()


def shards(section_modes, velocity, acceleration, species, neighbours, ghost_send):
    _, beads, atoms = section_modes.shape
    slots = neighbours.shape[0]
    ghosts = ghost_send.shape[1] // 2
    pad = -(-ghosts // 128) * 128
    rows = atoms + 2 * pad
    nbead, nslab = lax.axis_size("bead"), lax.axis_size("slab")
    sizes = (nbead, nslab, beads, atoms, ghosts, pad, slots)
    vmem = pl.BlockSpec(memory_space=pltpu.VMEM)
    result = jax.ShapeDtypeStruct(section_modes.shape, f32)
    dma = pltpu.SemaphoreType.DMA
    return pl.pallas_call(
        functools.partial(kernel, sizes),
        out_shape=(result, result, result),
        in_specs=[vmem] * 6,
        out_specs=(vmem, vmem, vmem),
        scratch_shapes=[
            pltpu.VMEM((slots, atoms), jnp.int32),
            pltpu.VMEM((slots, atoms), jnp.int32),
            pltpu.VMEM((rows, atoms), f32),
            pltpu.VMEM((3, beads, atoms), f32),
            pltpu.VMEM((atoms, 2 * pad), bf16),
            pltpu.VMEM((nbead, 8, rows), f32),
            pltpu.VMEM((8, 2 * pad), f32),
            pltpu.VMEM((8, rows), f32),
            pltpu.VMEM((rows, 8), f32),
            pltpu.VMEM((beads, rows, atoms), f32),
            pltpu.VMEM((beads, rows, atoms), f32),
            pltpu.VMEM((beads, rows, 128), f32),
            pltpu.VMEM((beads * 3, rows, 128), f32),
            pltpu.VMEM((beads, 8, 2 * pad), f32),
            pltpu.VMEM((beads, 8, 2 * pad), f32),
            pltpu.VMEM((beads, 8, 2 * pad), f32),
            pltpu.VMEM((beads, 8, 2 * pad), f32),
            pltpu.VMEM((beads, 8, atoms), f32),
            pltpu.VMEM((beads, rows, 8), f32),
            pltpu.VMEM((8, 2 * pad), f32),
            pltpu.VMEM((nbead, 8, rows), f32),
            pltpu.VMEM((8, rows), f32),
            dma((3 * nbead,)),
            dma((3 * nbead,)),
            dma((2 * beads,)),
            dma((2 * beads,)),
            dma((2 * beads,)),
            dma((2 * beads,)),
            dma((3 * nbead,)),
            dma((3 * nbead,)),
        ],
        compiler_params=pltpu.CompilerParams(
            collective_id=0, has_side_effects=True, vmem_limit_bytes=40 * 1024 * 1024
        ),
    )(
        section_modes,
        velocity,
        acceleration,
        species.reshape(1, atoms),
        neighbours,
        ghost_send,
    )


def solution(mesh):
    return jax.shard_map(
        shards,
        mesh=mesh,
        in_specs=(
            P(None, "bead", "slab"),
            P(None, "bead", "slab"),
            P(None, "bead", "slab"),
            P("slab"),
            P(None, "slab"),
            P("slab", None),
        ),
        out_specs=(P(None, "bead", "slab"), P(None, "bead", "slab"), P(None, "bead", "slab")),
        check_vma=False,
    )
```

```python
import functools
import math

import jax
import jax.numpy as jnp
import numpy as np
from jax import lax
from jax.experimental import pallas as pl
from jax.experimental.pallas import tpu as pltpu
from jax.sharding import PartitionSpec as P

step_dt = 0.1
spring = 6.0
alpha_shape = 0.3
beta_shape = 0.5
log2e = math.log2(math.e)
MESH = pl.DeviceIdType.MESH
f32 = jnp.float32
bf16 = jnp.bfloat16


def sectioning_inverse(number):
    row_table = np.zeros((number, number))
    row_table[0, 0] = 1.0
    for mode_level in range(number - 1, 0, -1):
        upper_row = row_table[0] if mode_level + 1 == number else row_table[mode_level + 1]
        row_table[mode_level] = (
            mode_level / (mode_level + 1.0) * upper_row + 1.0 / (mode_level + 1.0) * row_table[0]
        )
        row_table[mode_level, mode_level] += 1.0
    return row_table


def force_matrix(number):
    inverse = sectioning_inverse(number)
    weights = np.array([1.0] + [mode_level / (mode_level + 1.0) for mode_level in range(1, number)])
    return weights[:, None] * inverse.T / number


def split_rows(rows):
    high = rows.astype(bf16).astype(f32)
    rest = rows - high
    middle = rest.astype(bf16).astype(f32)
    return jnp.concatenate([high, middle, rest - middle], axis=0).astype(bf16)


def fold_pieces(product):
    return product[0:8] + product[8:16] + product[16:24]


def row_dot(rows, table):
    return fold_pieces(
        lax.dot_general(
            split_rows(rows), table, (((1,), (0,)), ((), ())), preferred_element_type=f32
        )
    )


def row_dot_nt(rows, table):
    return fold_pieces(
        lax.dot_general(
            split_rows(rows), table, (((1,), (1,)), ((), ())), preferred_element_type=f32
        )
    )


def lane_sums(selector, partial):
    high = partial.astype(bf16)
    rest = partial - high.astype(f32)
    middle = rest.astype(bf16)
    low = (rest - middle.astype(f32)).astype(bf16)
    total = None
    for piece in (high, middle, low):
        part = lax.dot_general(
            selector, piece, (((1,), (1,)), ((), ())), preferred_element_type=f32
        )
        total = part if total is None else total + part
    return total


def choose(index, table_values):
    value = f32(table_values[0])
    for i in range(1, len(table_values)):
        value = jnp.where(index == i, f32(table_values[i]), value)
    return value


def kernel(
    sizes,
    modes_in,
    vel_in,
    acc_in,
    spec_in,
    nb_in,
    ghost_in,
    out_modes,
    out_vel,
    out_acc,
    modes_ref,
    vel_ref,
    acc_ref,
    spec_ref,
    nb_ref,
    ghost_ref,
    sem_in,
    lo_ref,
    inc_ref,
    count_ref,
    turned_ref,
    onehot_ref,
    modes_all,
    send_modes,
    place_ref,
    column_ref,
    dens_ref,
    rep_ref,
    part_d,
    part_f,
    send_d,
    got_d,
    send_s,
    got_s,
    slope_ref,
    slope_col,
    send_f,
    force_all,
    mixed_ref,
    sem_a,
    rem_a,
    sem_b,
    rem_b,
    sem_c,
    rem_c,
    sem_f,
    rem_f,
):
    nbead, nslab, beads, atoms, ghosts, pad, slots = sizes
    number = nbead * beads
    b = lax.axis_index("bead")
    s = lax.axis_index("slab")
    left = lax.rem(s + nslab - 1, nslab)
    right = lax.rem(s + 1, nslab)

    loads = [
        pltpu.make_async_copy(src, dst, sem_in.at[i])
        for i, (src, dst) in enumerate(
            (
                (modes_in, modes_ref),
                (vel_in, vel_ref),
                (acc_in, acc_ref),
                (spec_in, spec_ref),
                (ghost_in, ghost_ref),
                (nb_in, nb_ref),
            )
        )
    ]
    for load in loads:
        load.start()
    barrier = pltpu.get_barrier_semaphore()
    peers = []
    for d in range(nbead):
        t = lax.rem(b + d, nbead)
        if d:
            peers.append((t, s))
        peers.append((t, left))
        peers.append((t, right))
    for peer in peers:
        pl.semaphore_signal(barrier, inc=1, device_id=peer, device_id_type=MESH)

    def remote(src, dst, sems, rems, index, device):
        return pltpu.make_async_remote_copy(
            src_ref=src,
            dst_ref=dst,
            send_sem=sems.at[index],
            recv_sem=rems.at[index],
            device_id=device,
            device_id_type=MESH,
        )

    for load in loads[:5]:
        load.wait()
    shape = (3, beads, atoms)
    first_mode = (lax.broadcasted_iota(jnp.int32, shape, 1) + b * beads) == 0
    modes = modes_ref[...]
    half_kick = vel_ref[...] + 0.5 * step_dt * acc_ref[...]
    angle = spring * step_dt
    cosine, sine = math.cos(angle), math.sin(angle)
    new_modes = jnp.where(
        first_mode, modes + step_dt * half_kick, cosine * modes + sine / spring * half_kick
    )
    turned_ref[...] = jnp.where(
        first_mode, half_kick, cosine * half_kick - spring * sine * modes
    )
    out_modes[...] = new_modes
    heavy = spec_ref[...] == 1
    for c in range(3):
        modes_all[b, c * beads : (c + 1) * beads, 0:atoms] = new_modes[c]
    modes_all[b, 6:7, 0:atoms] = jnp.where(heavy, f32(1.4), f32(0.6))
    modes_all[b, 7:8, 0:atoms] = jnp.where(heavy, f32(1.5), f32(0.8))

    listed = ghost_ref[...]
    lane = lax.broadcasted_iota(jnp.int32, (1, pad), 1)
    first_list = jnp.where(lane < ghosts, listed[:, 0:pad], -1)
    start = 2 * ghosts - pad
    second_list = jnp.where(
        lane < ghosts,
        pltpu.roll(
            jnp.broadcast_to(listed[:, start : start + pad], (8, pad)),
            pad - (ghosts - start),
            1,
        )[0:1],
        -1,
    )
    atom_ids = lax.broadcasted_iota(jnp.int32, (atoms, pad), 0)
    onehot_ref[:, 0:pad] = jnp.where(atom_ids == first_list, f32(1), f32(0)).astype(bf16)
    onehot_ref[:, pad : 2 * pad] = jnp.where(atom_ids == second_list, f32(1), f32(0)).astype(bf16)
    send_modes[...] = row_dot(modes_all[b, :, 0:atoms], onehot_ref[...])

    pl.semaphore_wait(barrier, len(peers))

    left_at = slice(atoms, atoms + pad)
    right_at = slice(atoms + pad, atoms + 2 * pad)

    def exchange(own_ref, src_left, src_right, buffer, at_left, at_right, sems, rems):
        copies = []
        for d in range(nbead):
            t = lax.rem(b + d, nbead)
            copies.append(
                remote(src_left, buffer.at[b, :, at_left], sems, rems, nbead + d, (t, left))
            )
            copies.append(
                remote(src_right, buffer.at[b, :, at_right], sems, rems, 2 * nbead + d, (t, right))
            )
            if d:
                copies.append(
                    remote(own_ref, buffer.at[b, :, 0:atoms], sems, rems, d, (t, s))
                )
        for copy in copies:
            copy.start()
        return copies

    copies_a = exchange(
        modes_all.at[b, :, 0:atoms],
        send_modes.at[:, 0:pad],
        send_modes.at[:, pad : 2 * pad],
        modes_all,
        right_at,
        left_at,
        sem_a,
        rem_a,
    )

    rows = atoms + 2 * pad
    field = rows // 4
    loads[5].wait()
    value = nb_ref[...]
    moved = jnp.where(
        value < ghosts,
        value + atoms,
        jnp.where(value < ghosts + atoms, value - ghosts, value - ghosts + pad),
    )
    level = (
        jnp.where(moved >= field, 1, 0)
        + jnp.where(moved >= 2 * field, 1, 0)
        + jnp.where(moved >= 3 * field, 1, 0)
    )
    lo_ref[...] = moved - level * field
    step = jnp.where(
        level == 0, 1, jnp.where(level == 1, 1 << 8, jnp.where(level == 2, 1 << 16, 1 << 24))
    )
    inc_ref[...] = jnp.where(value < atoms + 2 * ghosts, step, 0)
    group = 32
    row_ids = lax.broadcasted_iota(jnp.int32, (group, atoms), 0)

    def count_body(g, carry):
        base = g * group
        total = jnp.zeros((group, atoms), jnp.int32)
        for k in range(slots):
            total = total + jnp.where(
                row_ids == lo_ref[k : k + 1, :] - base, inc_ref[k : k + 1, :], 0
            )
        for level_id in range(4):
            at = pl.multiple_of(level_id * field + base, group)
            count_ref[pl.ds(at, group), :] = (
                (total >> (8 * level_id)) & 255
            ).astype(f32)
        return carry

    lax.fori_loop(0, field // group, count_body, 0)

    for side in range(2):
        at = atoms + side * pad + ghosts
        blank = jnp.zeros((pad - ghosts, 128), f32)
        for kk in range(beads):
            part_d[kk, at : at + pad - ghosts, :] = blank
            for c in range(3):
                part_f[kk * 3 + c, at : at + pad - ghosts, :] = blank

    sub_ids = lax.broadcasted_iota(jnp.int32, (8, 1), 0)

    def mix(buffer, matrix, kk):
        total = None
        for n in range(nbead):
            column = None
            for j in range(beads):
                coef = choose(
                    b, [matrix[i * beads + kk, n * beads + j] for i in range(nbead)]
                )
                column = (
                    jnp.full((8, 1), coef, f32)
                    if column is None
                    else jnp.where(lax.rem(sub_ids, beads) == j, coef, column)
                )
            part = column * buffer[n]
            total = part if total is None else total + part
        result = total
        for j in range(1, beads):
            result = result + pltpu.roll(total, 8 - j, 0)
        return result

    inverse = sectioning_inverse(number).astype(np.float32)
    for copy in copies_a:
        copy.wait_recv()
    place_ref[6:8, :] = modes_all[b, 6:8, :]
    for kk in range(beads):
        mixed = mix(modes_all, inverse, kk)
        for c in range(3):
            place_ref[kk * 3 + c : kk * 3 + c + 1, :] = mixed[c * beads : c * beads + 1, :]
    column_ref[...] = jnp.transpose(place_ref[...])

    def rows_of(index):
        return jnp.broadcast_to(place_ref[index : index + 1, 0:atoms], (8, atoms))

    def fold_lanes(full):
        out = full[:, 0:128]
        for at in range(128, atoms, 128):
            out = out + full[:, at : at + 128]
        return out

    unroll = 8

    def density_pass(kk, first_row, count, total):
        xn = [rows_of(kk * 3 + c) for c in range(3)]
        amp_n, rep_n = rows_of(6), rows_of(7)

        def body(i, total):
            for u in range(unroll):
                at = pl.multiple_of(first_row + (i * unroll + u) * 8, 8)
                here = pl.ds(at, 8)
                cols = column_ref[here, :]
                offset = [xn[c] - cols[:, kk * 3 + c : kk * 3 + c + 1] for c in range(3)]
                distance = (
                    offset[0] * offset[0] + offset[1] * offset[1] + offset[2] * offset[2]
                )
                listed_times = count_ref[here, :]
                dens = listed_times * jnp.exp2((-alpha_shape * log2e) * distance)
                repel = listed_times * jnp.exp2((-beta_shape * log2e) * distance)
                dens_ref[kk, here, :] = dens
                rep_ref[kk, here, :] = repel * (rep_n * cols[:, 7:8])
                part_d[kk, here, :] = fold_lanes(dens * amp_n)
                total = total + dens * cols[:, 6:7]
            return total

        return lax.fori_loop(0, count // (8 * unroll), body, total)

    ones = jnp.ones((8, 128), bf16)
    sides = (slice(atoms, atoms + pad), slice(atoms + pad, atoms + 2 * pad))
    totals = []
    copies_b = []
    for kk in range(beads):
        total = jnp.zeros((8, atoms), f32)
        for side in range(2):
            total = density_pass(kk, atoms + side * pad, ghosts, total)
            send_d[kk, :, side * pad : (side + 1) * pad] = lane_sums(
                ones, part_d[kk, sides[side], :]
            )
        pair = [
            remote(
                send_d.at[kk, :, 0:pad],
                got_d.at[kk, :, pad : 2 * pad],
                sem_b,
                rem_b,
                2 * kk,
                (b, left),
            ),
            remote(
                send_d.at[kk, :, pad : 2 * pad],
                got_d.at[kk, :, 0:pad],
                sem_b,
                rem_b,
                2 * kk + 1,
                (b, right),
            ),
        ]
        for copy in pair:
            copy.start()
        copies_b.append(pair)
        totals.append(total)
    locals_d = []
    for kk in range(beads):
        total = density_pass(kk, 0, atoms, totals[kk])
        locals_d.append(
            jnp.sum(total, axis=0, keepdims=True) + lane_sums(ones, part_d[kk, 0:atoms, :])
        )
    embed = jnp.where(heavy, f32(2.5), f32(1.0))
    copies_c = []
    for kk in range(beads):
        for copy in copies_b[kk]:
            copy.wait_recv()
        density = locals_d[kk] + row_dot_nt(got_d[kk], onehot_ref[...])
        slope = (-0.5 * 2.0 * alpha_shape) * embed / jnp.sqrt(1.0 + density)
        slope_ref[kk] = slope
        send_s[kk] = row_dot(slope, onehot_ref[...])
        pair = [
            remote(
                send_s.at[kk, :, 0:pad],
                got_s.at[kk, :, pad : 2 * pad],
                sem_c,
                rem_c,
                2 * kk,
                (b, left),
            ),
            remote(
                send_s.at[kk, :, pad : 2 * pad],
                got_s.at[kk, :, 0:pad],
                sem_c,
                rem_c,
                2 * kk + 1,
                (b, right),
            ),
        ]
        for copy in pair:
            copy.start()
        copies_c.append(pair)
        slope_col[kk, 0:atoms, :] = jnp.transpose(slope)

    def force_pass(kk, first_row, count, carry):
        xn = [rows_of(kk * 3 + c) for c in range(3)]
        amp_n = rows_of(6)
        slope_n = slope_ref[kk]

        def body(i, totals):
            for u in range(unroll):
                at = pl.multiple_of(first_row + (i * unroll + u) * 8, 8)
                here = pl.ds(at, 8)
                cols = column_ref[here, :]
                slope_m = slope_col[kk, here, :][:, 0:1]
                coupling = (
                    dens_ref[kk, here, :] * (slope_n * cols[:, 6:7] + amp_n * slope_m)
                    + rep_ref[kk, here, :]
                )
                out = []
                for c in range(3):
                    pair_force = coupling * (xn[c] - cols[:, kk * 3 + c : kk * 3 + c + 1])
                    part_f[kk * 3 + c, here, :] = fold_lanes(pair_force)
                    out.append(totals[c] + pair_force)
                totals = tuple(out)
            return totals

        return lax.fori_loop(0, count // (8 * unroll), body, carry)

    selector_ids = lax.broadcasted_iota(jnp.int32, (8, 128), 0)
    line_ids = lax.broadcasted_iota(jnp.int32, (8, atoms), 0)
    zero = jnp.zeros((8, atoms), f32)
    local_totals = [force_pass(kk, 0, atoms, (zero, zero, zero)) for kk in range(beads)]
    own = zero
    for kk in range(beads):
        for copy in copies_c[kk]:
            copy.wait_recv()
        slope_col[kk, atoms:rows, :] = jnp.transpose(got_s[kk])
        total = local_totals[kk]
        for side in range(2):
            total = force_pass(kk, atoms + side * pad, ghosts, total)
        for c in range(3):
            line = jnp.sum(total[c], axis=0, keepdims=True)
            own = own + jnp.where(line_ids == c * beads + kk, line, 0.0)
    sent = jnp.zeros((8, rows), f32)
    for kk in range(beads):
        for c in range(3):
            selector = jnp.where(selector_ids == c * beads + kk, f32(-1), f32(0)).astype(bf16)
            sent = sent + lane_sums(selector, part_f[kk * 3 + c])
    force_all[b, :, 0:atoms] = own + sent[:, 0:atoms]
    send_f[...] = sent[:, atoms:rows]
    copies_f = exchange(
        force_all.at[b, :, 0:atoms],
        send_f.at[:, 0:pad],
        send_f.at[:, pad : 2 * pad],
        force_all,
        right_at,
        left_at,
        sem_f,
        rem_f,
    )
    for copy in copies_a:
        copy.wait_send()
    for copy in sum(copies_b, []) + sum(copies_c, []):
        copy.wait_send()
    matrix = force_matrix(number).astype(np.float32)
    inverse_mass = jnp.where(heavy, f32(1.0 / 106.0), f32(1.0))
    for copy in copies_f:
        copy.wait_recv()
    mixed_ref[6:8, :] = jnp.zeros((2, rows), f32)
    for kk in range(beads):
        mixed = mix(force_all, matrix, kk)
        for c in range(3):
            at = c * beads + kk
            mixed_ref[at : at + 1, :] = mixed[c * beads : c * beads + 1, :]
    accel = (
        mixed_ref[:, 0:atoms] + row_dot_nt(mixed_ref[:, atoms:rows], onehot_ref[...])
    ) * inverse_mass
    for c in range(3):
        piece = accel[c * beads : (c + 1) * beads]
        out_acc[c] = piece
        out_vel[c] = turned_ref[c] + 0.5 * step_dt * piece
    for copy in copies_f:
        copy.wait_send()


def store_kernel(a_in, b_in, c_in, a_out, b_out, c_out, sems):
    copies = [
        pltpu.make_async_copy(src, dst, sems.at[i])
        for i, (src, dst) in enumerate(((a_in, a_out), (b_in, b_out), (c_in, c_out)))
    ]
    for copy in copies:
        copy.start()
    for copy in copies:
        copy.wait()


def shards(section_modes, velocity, acceleration, species, neighbours, ghost_send):
    _, beads, atoms = section_modes.shape
    slots = neighbours.shape[0]
    ghosts = ghost_send.shape[1] // 2
    pad = -(-ghosts // 128) * 128
    rows = atoms + 2 * pad
    nbead, nslab = lax.axis_size("bead"), lax.axis_size("slab")
    sizes = (nbead, nslab, beads, atoms, ghosts, pad, slots)
    vmem = pl.BlockSpec(memory_space=pltpu.VMEM)
    result = jax.ShapeDtypeStruct(section_modes.shape, f32)
    dma = pltpu.SemaphoreType.DMA
    results = pl.pallas_call(
        functools.partial(kernel, sizes),
        out_shape=(result, result, result),
        in_specs=[pl.BlockSpec(memory_space=pltpu.HBM)] * 6,
        out_specs=(vmem, vmem, vmem),
        scratch_shapes=[
            pltpu.VMEM(section_modes.shape, f32),
            pltpu.VMEM(section_modes.shape, f32),
            pltpu.VMEM(section_modes.shape, f32),
            pltpu.VMEM((1, atoms), jnp.int32),
            pltpu.VMEM((slots, atoms), jnp.int32),
            pltpu.VMEM((1, 2 * ghosts), jnp.int32),
            dma((6,)),
            pltpu.VMEM((slots, atoms), jnp.int32),
            pltpu.VMEM((slots, atoms), jnp.int32),
            pltpu.VMEM((rows, atoms), f32),
            pltpu.VMEM((3, beads, atoms), f32),
            pltpu.VMEM((atoms, 2 * pad), bf16),
            pltpu.VMEM((nbead, 8, rows), f32),
            pltpu.VMEM((8, 2 * pad), f32),
            pltpu.VMEM((8, rows), f32),
            pltpu.VMEM((rows, 8), f32),
            pltpu.VMEM((beads, rows, atoms), f32),
            pltpu.VMEM((beads, rows, atoms), f32),
            pltpu.VMEM((beads, rows, 128), f32),
            pltpu.VMEM((beads * 3, rows, 128), f32),
            pltpu.VMEM((beads, 8, 2 * pad), f32),
            pltpu.VMEM((beads, 8, 2 * pad), f32),
            pltpu.VMEM((beads, 8, 2 * pad), f32),
            pltpu.VMEM((beads, 8, 2 * pad), f32),
            pltpu.VMEM((beads, 8, atoms), f32),
            pltpu.VMEM((beads, rows, 8), f32),
            pltpu.VMEM((8, 2 * pad), f32),
            pltpu.VMEM((nbead, 8, rows), f32),
            pltpu.VMEM((8, rows), f32),
            dma((3 * nbead,)),
            dma((3 * nbead,)),
            dma((2 * beads,)),
            dma((2 * beads,)),
            dma((2 * beads,)),
            dma((2 * beads,)),
            dma((3 * nbead,)),
            dma((3 * nbead,)),
        ],
        compiler_params=pltpu.CompilerParams(
            collective_id=0, has_side_effects=True, vmem_limit_bytes=64 * 1024 * 1024
        ),
    )(
        section_modes,
        velocity,
        acceleration,
        species.reshape(1, atoms),
        neighbours,
        ghost_send,
    )
    return pl.pallas_call(
        store_kernel,
        out_shape=(result, result, result),
        in_specs=[vmem] * 3,
        out_specs=[pl.BlockSpec(memory_space=pltpu.HBM)] * 3,
        scratch_shapes=[dma((3,))],
        compiler_params=pltpu.CompilerParams(vmem_limit_bytes=64 * 1024 * 1024),
    )(*results)


def solution(mesh):
    return jax.shard_map(
        shards,
        mesh=mesh,
        in_specs=(
            P(None, "bead", "slab"),
            P(None, "bead", "slab"),
            P(None, "bead", "slab"),
            P("slab"),
            P(None, "slab"),
            P("slab", None),
        ),
        out_specs=(P(None, "bead", "slab"), P(None, "bead", "slab"), P(None, "bead", "slab")),
        check_vma=False,
    )
```

```python
import functools
import math

import jax
import jax.numpy as jnp
import numpy as np
from jax import lax
from jax.experimental import pallas as pl
from jax.experimental.pallas import tpu as pltpu
from jax.sharding import PartitionSpec as P

step_dt = 0.1
spring = 6.0
alpha_shape = 0.3
beta_shape = 0.5
log2e = math.log2(math.e)
MESH = pl.DeviceIdType.MESH
f32 = jnp.float32
bf16 = jnp.bfloat16


def sectioning_inverse(number):
    row_table = np.zeros((number, number))
    row_table[0, 0] = 1.0
    for mode_level in range(number - 1, 0, -1):
        upper_row = row_table[0] if mode_level + 1 == number else row_table[mode_level + 1]
        row_table[mode_level] = (
            mode_level / (mode_level + 1.0) * upper_row + 1.0 / (mode_level + 1.0) * row_table[0]
        )
        row_table[mode_level, mode_level] += 1.0
    return row_table


def force_matrix(number):
    inverse = sectioning_inverse(number)
    weights = np.array([1.0] + [mode_level / (mode_level + 1.0) for mode_level in range(1, number)])
    return weights[:, None] * inverse.T / number


def split_rows(rows):
    high = rows.astype(bf16).astype(f32)
    rest = rows - high
    middle = rest.astype(bf16).astype(f32)
    return jnp.concatenate([high, middle, rest - middle], axis=0).astype(bf16)


def fold_pieces(product):
    return product[0:8] + product[8:16] + product[16:24]


def row_dot(rows, table):
    return fold_pieces(
        lax.dot_general(
            split_rows(rows), table, (((1,), (0,)), ((), ())), preferred_element_type=f32
        )
    )


def row_dot_nt(rows, table):
    return fold_pieces(
        lax.dot_general(
            split_rows(rows), table, (((1,), (1,)), ((), ())), preferred_element_type=f32
        )
    )


def lane_sums(selector, partial):
    high = partial.astype(bf16)
    rest = partial - high.astype(f32)
    middle = rest.astype(bf16)
    total = None
    for piece in (high, middle):
        part = lax.dot_general(
            selector, piece, (((1,), (1,)), ((), ())), preferred_element_type=f32
        )
        total = part if total is None else total + part
    return total


def choose(index, table_values):
    value = f32(table_values[0])
    for i in range(1, len(table_values)):
        value = jnp.where(index == i, f32(table_values[i]), value)
    return value


def kernel(
    sizes,
    modes_in,
    vel_in,
    acc_in,
    spec_in,
    nb_in,
    ghost_in,
    out_modes,
    out_vel,
    out_acc,
    modes_ref,
    vel_ref,
    acc_ref,
    spec_ref,
    nb_ref,
    ghost_ref,
    sem_in,
    lo_ref,
    inc_ref,
    count_ref,
    turned_ref,
    onehot_ref,
    modes_all,
    send_modes,
    place_ref,
    column_ref,
    dens_ref,
    rep_ref,
    part_d,
    part_f,
    send_d,
    got_d,
    send_s,
    got_s,
    slope_ref,
    slope_col,
    send_f,
    force_all,
    mixed_ref,
    sem_a,
    rem_a,
    sem_b,
    rem_b,
    sem_c,
    rem_c,
    sem_f,
    rem_f,
):
    nbead, nslab, beads, atoms, ghosts, pad, slots = sizes
    number = nbead * beads
    b = lax.axis_index("bead")
    s = lax.axis_index("slab")
    left = lax.rem(s + nslab - 1, nslab)
    right = lax.rem(s + 1, nslab)

    loads = [
        pltpu.make_async_copy(src, dst, sem_in.at[i])
        for i, (src, dst) in enumerate(
            (
                (modes_in, modes_ref),
                (vel_in, vel_ref),
                (acc_in, acc_ref),
                (spec_in, spec_ref),
                (ghost_in, ghost_ref),
                (nb_in, nb_ref),
            )
        )
    ]
    for load in loads:
        load.start()
    barrier = pltpu.get_barrier_semaphore()
    peers = []
    for d in range(nbead):
        t = lax.rem(b + d, nbead)
        if d:
            peers.append((t, s))
        peers.append((t, left))
        peers.append((t, right))
    for peer in peers:
        pl.semaphore_signal(barrier, inc=1, device_id=peer, device_id_type=MESH)

    def remote(src, dst, sems, rems, index, device):
        return pltpu.make_async_remote_copy(
            src_ref=src,
            dst_ref=dst,
            send_sem=sems.at[index],
            recv_sem=rems.at[index],
            device_id=device,
            device_id_type=MESH,
        )

    for load in loads[:5]:
        load.wait()
    shape = (3, beads, atoms)
    first_mode = (lax.broadcasted_iota(jnp.int32, shape, 1) + b * beads) == 0
    modes = modes_ref[...]
    half_kick = vel_ref[...] + 0.5 * step_dt * acc_ref[...]
    angle = spring * step_dt
    cosine, sine = math.cos(angle), math.sin(angle)
    new_modes = jnp.where(
        first_mode, modes + step_dt * half_kick, cosine * modes + sine / spring * half_kick
    )
    turned_ref[...] = jnp.where(
        first_mode, half_kick, cosine * half_kick - spring * sine * modes
    )
    out_modes[...] = new_modes
    heavy = spec_ref[...] == 1
    for c in range(3):
        modes_all[b, c * beads : (c + 1) * beads, 0:atoms] = new_modes[c]
    modes_all[b, 6:7, 0:atoms] = jnp.where(heavy, f32(1.4), f32(0.6))
    modes_all[b, 7:8, 0:atoms] = jnp.where(heavy, f32(1.5), f32(0.8))

    listed = ghost_ref[...]
    lane = lax.broadcasted_iota(jnp.int32, (1, pad), 1)
    first_list = jnp.where(lane < ghosts, listed[:, 0:pad], -1)
    start = 2 * ghosts - pad
    second_list = jnp.where(
        lane < ghosts,
        pltpu.roll(
            jnp.broadcast_to(listed[:, start : start + pad], (8, pad)),
            pad - (ghosts - start),
            1,
        )[0:1],
        -1,
    )
    atom_ids = lax.broadcasted_iota(jnp.int32, (atoms, pad), 0)
    onehot_ref[:, 0:pad] = jnp.where(atom_ids == first_list, f32(1), f32(0)).astype(bf16)
    onehot_ref[:, pad : 2 * pad] = jnp.where(atom_ids == second_list, f32(1), f32(0)).astype(bf16)
    send_modes[...] = row_dot(modes_all[b, :, 0:atoms], onehot_ref[...])

    pl.semaphore_wait(barrier, len(peers))

    left_at = slice(atoms, atoms + pad)
    right_at = slice(atoms + pad, atoms + 2 * pad)

    def exchange(own_ref, src_left, src_right, buffer, at_left, at_right, sems, rems):
        copies = []
        for d in range(nbead):
            t = lax.rem(b + d, nbead)
            copies.append(
                remote(src_left, buffer.at[b, :, at_left], sems, rems, nbead + d, (t, left))
            )
            copies.append(
                remote(src_right, buffer.at[b, :, at_right], sems, rems, 2 * nbead + d, (t, right))
            )
            if d:
                copies.append(
                    remote(own_ref, buffer.at[b, :, 0:atoms], sems, rems, d, (t, s))
                )
        for copy in copies:
            copy.start()
        return copies

    copies_a = exchange(
        modes_all.at[b, :, 0:atoms],
        send_modes.at[:, 0:pad],
        send_modes.at[:, pad : 2 * pad],
        modes_all,
        right_at,
        left_at,
        sem_a,
        rem_a,
    )

    rows = atoms + 2 * pad
    field = rows // 4
    loads[5].wait()
    value = nb_ref[...]
    moved = jnp.where(
        value < ghosts,
        value + atoms,
        jnp.where(value < ghosts + atoms, value - ghosts, value - ghosts + pad),
    )
    level = (
        jnp.where(moved >= field, 1, 0)
        + jnp.where(moved >= 2 * field, 1, 0)
        + jnp.where(moved >= 3 * field, 1, 0)
    )
    lo_ref[...] = moved - level * field
    step = jnp.where(
        level == 0, 1, jnp.where(level == 1, 1 << 8, jnp.where(level == 2, 1 << 16, 1 << 24))
    )
    inc_ref[...] = jnp.where(value < atoms + 2 * ghosts, step, 0)
    group = 32
    row_ids = lax.broadcasted_iota(jnp.int32, (group, atoms), 0)

    def count_body(g, carry):
        base = g * group
        total = jnp.zeros((group, atoms), jnp.int32)
        for k in range(slots):
            total = total + jnp.where(
                row_ids == lo_ref[k : k + 1, :] - base, inc_ref[k : k + 1, :], 0
            )
        for level_id in range(4):
            at = pl.multiple_of(level_id * field + base, group)
            count_ref[pl.ds(at, group), :] = (
                (total >> (8 * level_id)) & 255
            ).astype(f32)
        return carry

    lax.fori_loop(0, field // group, count_body, 0)

    for side in range(2):
        at = atoms + side * pad + ghosts
        blank = jnp.zeros((pad - ghosts, 128), f32)
        for kk in range(beads):
            part_d[kk, at : at + pad - ghosts, :] = blank
            for c in range(3):
                part_f[kk * 3 + c, at : at + pad - ghosts, :] = blank

    sub_ids = lax.broadcasted_iota(jnp.int32, (8, 1), 0)

    def mix_columns(matrix, kk):
        columns = []
        for n in range(nbead):
            column = None
            for j in range(beads):
                coef = choose(
                    b, [matrix[i * beads + kk, n * beads + j] for i in range(nbead)]
                )
                column = (
                    jnp.full((8, 1), coef, f32)
                    if column is None
                    else jnp.where(lax.rem(sub_ids, beads) == j, coef, column)
                )
            columns.append(column)
        return columns

    def mix(buffer, columns):
        total = None
        for n in range(nbead):
            part = columns[n] * buffer[n]
            total = part if total is None else total + part
        result = total
        for j in range(1, beads):
            result = result + pltpu.roll(total, 8 - j, 0)
        return result

    inverse = sectioning_inverse(number).astype(np.float32)
    inverse_columns = [mix_columns(inverse, kk) for kk in range(beads)]
    for copy in copies_a:
        copy.wait_recv()
    place_ref[6:8, :] = modes_all[b, 6:8, :]
    for kk in range(beads):
        mixed = mix(modes_all, inverse_columns[kk])
        for c in range(3):
            place_ref[kk * 3 + c : kk * 3 + c + 1, :] = mixed[c * beads : c * beads + 1, :]
    column_ref[...] = jnp.transpose(place_ref[...])

    def rows_of(index):
        return jnp.broadcast_to(place_ref[index : index + 1, 0:atoms], (8, atoms))

    def fold_lanes(full):
        out = full[:, 0:128]
        for at in range(128, atoms, 128):
            out = out + full[:, at : at + 128]
        return out

    unroll = 8

    def density_pass(kk, first_row, count, total):
        unroll = 32 if count % 256 == 0 else 24 if count % 192 == 0 else 8
        xn = [rows_of(kk * 3 + c) for c in range(3)]
        amp_n, rep_n = rows_of(6), rows_of(7)

        def body(i, total):
            for u in range(unroll):
                at = pl.multiple_of(first_row + (i * unroll + u) * 8, 8)
                here = pl.ds(at, 8)
                cols = column_ref[here, :]
                offset = [xn[c] - cols[:, kk * 3 + c : kk * 3 + c + 1] for c in range(3)]
                distance = (
                    offset[0] * offset[0] + offset[1] * offset[1] + offset[2] * offset[2]
                )
                listed_times = count_ref[here, :]
                dens = listed_times * jnp.exp2((-alpha_shape * log2e) * distance)
                repel = listed_times * jnp.exp2((-beta_shape * log2e) * distance)
                dens_ref[kk, here, :] = dens
                rep_ref[kk, here, :] = repel * (rep_n * cols[:, 7:8])
                part_d[kk, here, :] = fold_lanes(dens * amp_n)
                total = total + dens * cols[:, 6:7]
            return total

        return lax.fori_loop(0, count // (8 * unroll), body, total)

    ones = jnp.ones((8, 128), bf16)
    sides = (slice(atoms, atoms + pad), slice(atoms + pad, atoms + 2 * pad))
    totals = []
    copies_b = []
    for kk in range(beads):
        total = jnp.zeros((8, atoms), f32)
        for side in range(2):
            total = density_pass(kk, atoms + side * pad, ghosts, total)
            send_d[kk, :, side * pad : (side + 1) * pad] = lane_sums(
                ones, part_d[kk, sides[side], :]
            )
        pair = [
            remote(
                send_d.at[kk, :, 0:pad],
                got_d.at[kk, :, pad : 2 * pad],
                sem_b,
                rem_b,
                2 * kk,
                (b, left),
            ),
            remote(
                send_d.at[kk, :, pad : 2 * pad],
                got_d.at[kk, :, 0:pad],
                sem_b,
                rem_b,
                2 * kk + 1,
                (b, right),
            ),
        ]
        for copy in pair:
            copy.start()
        copies_b.append(pair)
        totals.append(total)
    locals_d = []
    for kk in range(beads):
        total = density_pass(kk, 0, atoms, totals[kk])
        locals_d.append(
            jnp.sum(total, axis=0, keepdims=True) + lane_sums(ones, part_d[kk, 0:atoms, :])
        )
    embed = jnp.where(heavy, f32(2.5), f32(1.0))
    copies_c = []
    for kk in range(beads):
        for copy in copies_b[kk]:
            copy.wait_recv()
        density = locals_d[kk] + row_dot_nt(got_d[kk], onehot_ref[...])
        slope = (-0.5 * 2.0 * alpha_shape) * embed / jnp.sqrt(1.0 + density)
        slope_ref[kk] = slope
        send_s[kk] = row_dot(slope, onehot_ref[...])
        pair = [
            remote(
                send_s.at[kk, :, 0:pad],
                got_s.at[kk, :, pad : 2 * pad],
                sem_c,
                rem_c,
                2 * kk,
                (b, left),
            ),
            remote(
                send_s.at[kk, :, pad : 2 * pad],
                got_s.at[kk, :, 0:pad],
                sem_c,
                rem_c,
                2 * kk + 1,
                (b, right),
            ),
        ]
        for copy in pair:
            copy.start()
        copies_c.append(pair)
        slope_col[kk, 0:atoms, :] = jnp.transpose(slope)

    def force_pass(kk, first_row, count, carry):
        unroll = 32 if count % 256 == 0 else 24 if count % 192 == 0 else 8
        xn = [rows_of(kk * 3 + c) for c in range(3)]
        amp_n = rows_of(6)
        slope_n = slope_ref[kk]

        def body(i, totals):
            for u in range(unroll):
                at = pl.multiple_of(first_row + (i * unroll + u) * 8, 8)
                here = pl.ds(at, 8)
                cols = column_ref[here, :]
                slope_m = slope_col[kk, here, :][:, 0:1]
                coupling = (
                    dens_ref[kk, here, :] * (slope_n * cols[:, 6:7] + amp_n * slope_m)
                    + rep_ref[kk, here, :]
                )
                out = []
                for c in range(3):
                    pair_force = coupling * (xn[c] - cols[:, kk * 3 + c : kk * 3 + c + 1])
                    part_f[kk * 3 + c, here, :] = fold_lanes(pair_force)
                    out.append(totals[c] + pair_force)
                totals = tuple(out)
            return totals

        return lax.fori_loop(0, count // (8 * unroll), body, carry)

    selector_ids = lax.broadcasted_iota(jnp.int32, (8, 128), 0)
    line_ids = lax.broadcasted_iota(jnp.int32, (8, atoms), 0)
    zero = jnp.zeros((8, atoms), f32)
    local_totals = [force_pass(kk, 0, atoms, (zero, zero, zero)) for kk in range(beads)]
    def lane_rows(at, into):
        for kk in range(beads):
            for c in range(3):
                selector = jnp.where(selector_ids == c * beads + kk, f32(-1), f32(0)).astype(bf16)
                into = into + lane_sums(selector, part_f[kk * 3 + c, at, :])
        return into

    own = lane_rows(slice(0, atoms), zero)
    for kk in range(beads):
        for copy in copies_c[kk]:
            copy.wait_recv()
        slope_col[kk, atoms:rows, :] = jnp.transpose(got_s[kk])
        total = local_totals[kk]
        for side in range(2):
            total = force_pass(kk, atoms + side * pad, ghosts, total)
        for c in range(3):
            line = jnp.sum(total[c], axis=0, keepdims=True)
            own = own + jnp.where(line_ids == c * beads + kk, line, 0.0)
    force_all[b, :, 0:atoms] = own
    send_f[...] = lane_rows(slice(atoms, rows), jnp.zeros((8, 2 * pad), f32))
    copies_f = exchange(
        force_all.at[b, :, 0:atoms],
        send_f.at[:, 0:pad],
        send_f.at[:, pad : 2 * pad],
        force_all,
        right_at,
        left_at,
        sem_f,
        rem_f,
    )
    for copy in copies_a:
        copy.wait_send()
    for copy in sum(copies_b, []) + sum(copies_c, []):
        copy.wait_send()
    matrix = force_matrix(number).astype(np.float32)
    force_columns = [mix_columns(matrix, kk) for kk in range(beads)]
    inverse_mass = jnp.where(heavy, f32(1.0 / 106.0), f32(1.0))
    for copy in copies_f:
        copy.wait_recv()
    mixed_ref[6:8, :] = jnp.zeros((2, rows), f32)
    for kk in range(beads):
        mixed = mix(force_all, force_columns[kk])
        for c in range(3):
            at = c * beads + kk
            mixed_ref[at : at + 1, :] = mixed[c * beads : c * beads + 1, :]
    accel = (
        mixed_ref[:, 0:atoms] + row_dot_nt(mixed_ref[:, atoms:rows], onehot_ref[...])
    ) * inverse_mass
    for c in range(3):
        piece = accel[c * beads : (c + 1) * beads]
        out_acc[c] = piece
        out_vel[c] = turned_ref[c] + 0.5 * step_dt * piece
    for copy in copies_f:
        copy.wait_send()


def store_kernel(a_in, b_in, c_in, a_out, b_out, c_out, sems):
    copies = [
        pltpu.make_async_copy(src, dst, sems.at[i])
        for i, (src, dst) in enumerate(((a_in, a_out), (b_in, b_out), (c_in, c_out)))
    ]
    for copy in copies:
        copy.start()
    for copy in copies:
        copy.wait()


def shards(section_modes, velocity, acceleration, species, neighbours, ghost_send):
    _, beads, atoms = section_modes.shape
    slots = neighbours.shape[0]
    ghosts = ghost_send.shape[1] // 2
    pad = -(-ghosts // 128) * 128
    rows = atoms + 2 * pad
    nbead, nslab = lax.axis_size("bead"), lax.axis_size("slab")
    sizes = (nbead, nslab, beads, atoms, ghosts, pad, slots)
    vmem = pl.BlockSpec(memory_space=pltpu.VMEM)
    result = jax.ShapeDtypeStruct(section_modes.shape, f32)
    dma = pltpu.SemaphoreType.DMA
    results = pl.pallas_call(
        functools.partial(kernel, sizes),
        out_shape=(result, result, result),
        in_specs=[pl.BlockSpec(memory_space=pltpu.HBM)] * 6,
        out_specs=(vmem, vmem, vmem),
        scratch_shapes=[
            pltpu.VMEM(section_modes.shape, f32),
            pltpu.VMEM(section_modes.shape, f32),
            pltpu.VMEM(section_modes.shape, f32),
            pltpu.VMEM((1, atoms), jnp.int32),
            pltpu.VMEM((slots, atoms), jnp.int32),
            pltpu.VMEM((1, 2 * ghosts), jnp.int32),
            dma((6,)),
            pltpu.VMEM((slots, atoms), jnp.int32),
            pltpu.VMEM((slots, atoms), jnp.int32),
            pltpu.VMEM((rows, atoms), f32),
            pltpu.VMEM((3, beads, atoms), f32),
            pltpu.VMEM((atoms, 2 * pad), bf16),
            pltpu.VMEM((nbead, 8, rows), f32),
            pltpu.VMEM((8, 2 * pad), f32),
            pltpu.VMEM((8, rows), f32),
            pltpu.VMEM((rows, 8), f32),
            pltpu.VMEM((beads, rows, atoms), f32),
            pltpu.VMEM((beads, rows, atoms), f32),
            pltpu.VMEM((beads, rows, 128), f32),
            pltpu.VMEM((beads * 3, rows, 128), f32),
            pltpu.VMEM((beads, 8, 2 * pad), f32),
            pltpu.VMEM((beads, 8, 2 * pad), f32),
            pltpu.VMEM((beads, 8, 2 * pad), f32),
            pltpu.VMEM((beads, 8, 2 * pad), f32),
            pltpu.VMEM((beads, 8, atoms), f32),
            pltpu.VMEM((beads, rows, 8), f32),
            pltpu.VMEM((8, 2 * pad), f32),
            pltpu.VMEM((nbead, 8, rows), f32),
            pltpu.VMEM((8, rows), f32),
            dma((3 * nbead,)),
            dma((3 * nbead,)),
            dma((2 * beads,)),
            dma((2 * beads,)),
            dma((2 * beads,)),
            dma((2 * beads,)),
            dma((3 * nbead,)),
            dma((3 * nbead,)),
        ],
        compiler_params=pltpu.CompilerParams(
            collective_id=0, has_side_effects=True, vmem_limit_bytes=64 * 1024 * 1024
        ),
    )(
        section_modes,
        velocity,
        acceleration,
        species.reshape(1, atoms),
        neighbours,
        ghost_send,
    )
    return pl.pallas_call(
        store_kernel,
        out_shape=(result, result, result),
        in_specs=[vmem] * 3,
        out_specs=[pl.BlockSpec(memory_space=pltpu.HBM)] * 3,
        scratch_shapes=[dma((3,))],
        compiler_params=pltpu.CompilerParams(vmem_limit_bytes=64 * 1024 * 1024),
    )(*results)


def solution(mesh):
    return jax.shard_map(
        shards,
        mesh=mesh,
        in_specs=(
            P(None, "bead", "slab"),
            P(None, "bead", "slab"),
            P(None, "bead", "slab"),
            P("slab"),
            P(None, "slab"),
            P("slab", None),
        ),
        out_specs=(P(None, "bead", "slab"), P(None, "bead", "slab"), P(None, "bead", "slab")),
        check_vma=False,
    )
```
